256 devices in a mesh: blk: 32 (over z, x_lo, core), pool: 8 (over x_hi, y).
Axes of the slice: x: 4 (x_hi: 2, x_lo: 2; x = x_hi * 2 + x_lo), y: 4, z: 8, core: 2. Of those that a mesh axis runs over, the one named last changes fastest.
Arguments:
- queries: bfloat16 [256, 128, 128], P('blk', 'pool'), may hold values from -5 to 5
- kv_cache: bfloat16 [8, 6144, 16, 256], P(None, ('blk', 'pool')), may hold values from -6 to 6
- block_owner: int32 [3072, 1], P('blk'), may hold values from 0 to 7; in each aligned block of 96 rows (0 to 95, 96 to 191, ...) at most 24 rows name the same one
Outputs:
- attended: bfloat16 [256, 128, 128], P('blk', 'pool')
The draws below stay inside these ranges and needn't reach their ends.
Inputs may be any that keep to these rules, and one draw needn't show every extreme that they name: `block_owner`: in the rows of one holder (aligned blocks of 96 rows) no owner is named more than 24 times; in some holders one owner is named exactly 24 times.
All inputs are finite; a program needn't handle non-finite values.
Results may differ from the reference program's by a relative error of at most 0.0047.
Values may be sent and summed in bfloat16 or wider, within the bound.
A program may use at most 64 MiB of HBM per device.

```python
import math
import jax
import jax.numpy as jnp
import numpy as np
from jax import lax

QH = 128
KVH = 8
HEAD_SIZE = 128
BS = 16
NB = 96
GROUP = 16
REQUESTS = 256
CAP = 24
SLOTS = 6144
BLOCKS = 3072
N_BLK = 32
N_POOL = 8


def draw_queries(key, part):
    key = jax.random.fold_in(key, 11)
    shape = (REQUESTS, QH, HEAD_SIZE)
    return jnp.clip(jax.random.normal(key, shape, jnp.float32), -5.0, 5.0).astype(jnp.bfloat16)


def draw_kv_cache(key, part):
    key = jax.random.fold_in(key, 12)
    shape = (KVH, SLOTS, BS, 2 * HEAD_SIZE)
    return jnp.clip(jax.random.normal(key, shape, jnp.float32), -6.0, 6.0).astype(jnp.bfloat16)


def assign_block(key, own, number, rows, number_of, top, reach, skew):
    sequence = jax.random.permutation(key, number_of)
    heavy_load, ordinary = shares(number_of, rows * top, reach, skew, True), shares(number_of, rows * top, reach, skew, False)
    places = jnp.arange(number_of)

    def named(sizes, offset_by):
        used = int((sizes > 0).sum())
        fixed = max(1, used // 4)
        passed = fixed + (places - fixed + offset_by * (used - fixed)) % max(1, number_of - fixed)
        return jnp.zeros((number_of,), jnp.int32).at[sequence[jnp.where(places < fixed, places, passed)]].set(jnp.asarray(sizes, jnp.int32))

    sizes = jnp.where(number % 4 == 0, named(heavy_load, number // 4), named(ordinary, number - number // 4 - 1))
    mixed = jax.random.permutation(jax.random.fold_in(own, 3), number_of)
    donor, receiver = mixed[0:number_of // 2 * 2:2], mixed[1:number_of // 2 * 2:2]
    room = jnp.minimum(sizes[donor] - 1, reach - sizes[receiver]) // 2
    room = jnp.where((donor == sequence[0]) | (receiver == sequence[0]) | (sizes[receiver] == 0), 0, jnp.maximum(room, 0))
    passed = jax.random.randint(jax.random.fold_in(own, 4), (number_of // 2,), 0, 1 << 20) % (room + 1)
    sizes = sizes.at[donor].add(-passed).at[receiver].add(passed)
    members = jnp.searchsorted(jnp.cumsum(sizes), jnp.arange(rows * top), side="right").astype(jnp.int32)
    listing = members.reshape(top, rows).T
    listing = listing[jax.random.permutation(jax.random.fold_in(own, 1), rows)]
    offset_by = jax.random.randint(jax.random.fold_in(own, 2), (rows, 1), 0, top)
    return jnp.take_along_axis(listing, (jnp.arange(top)[None, :] + offset_by) % top, axis=1)


def shares(amount, total, reach, slope, full):
    loads = [(1 << 20) // math.isqrt(grade ** slope) + 1 for grade in range(1, amount + 1)]
    largest = reach if full else min(reach, max(-(-total // amount), total * loads[0] // sum(loads)))
    least = 1 if total - largest >= amount - 1 else 0
    given, surplus = [largest] + [least] * (amount - 1), total - largest - least * (amount - 1)
    while surplus > 0:
        movable = [i for i in range(1, amount) if given[i] < largest] or [i for i in range(1, amount) if given[i] < reach]
        whole, left = sum([loads[i] for i in movable]), surplus
        for i in movable:
            more = min(reach - given[i], max(1, left * loads[i] // whole), surplus)
            given[i] = given[i] + more
            surplus = surplus - more
    return np.array(given)


def setup_inputs(seed: int = 0) -> dict:
    seeds = jax.random.split(jax.random.key(seed), 4)
    queries = draw_queries(jax.random.fold_in(seeds[3], 71), 0)
    kv_cache = draw_kv_cache(jax.random.fold_in(seeds[3], 71), 0)
    block_owner_keys = jax.random.split(jax.random.fold_in(seeds[2], 1), BLOCKS // NB)
    block_owner_turns = jax.random.permutation(jax.random.fold_in(seeds[2], 3), BLOCKS // NB)
    block_owner = jax.vmap(lambda own, number: assign_block(jax.random.fold_in(seeds[2], 2), own, number, NB, N_POOL, 1, CAP, 2))(block_owner_keys, block_owner_turns).reshape((BLOCKS, 1))
    return dict(queries=queries, kv_cache=kv_cache, block_owner=block_owner)


def holder_prefix(kv_cache, block_owner, holder):
    owner_ids = lax.dynamic_slice_in_dim(block_owner[:, 0], holder * NB, NB)
    onehot = (owner_ids[:, None] == jnp.arange(N_POOL, dtype=jnp.int32)[None, :]).astype(jnp.int32)
    earlier = jnp.cumsum(onehot, axis=0) - onehot
    slot_rank = lax.optimization_barrier(jnp.sum(earlier * onehot, axis=1))
    slot_ids = ((holder * N_POOL + owner_ids) * CAP + slot_rank).astype(jnp.int32)
    blocks = jnp.take(kv_cache, slot_ids, axis=1)
    return blocks.reshape(KVH, NB * BS, 2 * HEAD_SIZE)

def reference(queries, kv_cache, block_owner):
    query_matrix = queries.astype(jnp.float32).reshape(REQUESTS, KVH, GROUP, HEAD_SIZE).transpose(1, 0, 2, 3)
    query_matrix = query_matrix.reshape(KVH, REQUESTS * GROUP, HEAD_SIZE)
    logit_scale = 1.0 / math.sqrt(HEAD_SIZE)

    def visit(running, holder):
        common_prefix = holder_prefix(kv_cache, block_owner, holder).astype(jnp.float32)
        attention_logits = jnp.einsum('hun,hwn->huw', query_matrix, common_prefix[:, :, :HEAD_SIZE]) * logit_scale
        maxima = lax.optimization_barrier(jnp.max(attention_logits, axis=-1))
        exponent = jnp.exp(attention_logits - maxima[..., None])
        totals = lax.optimization_barrier(jnp.sum(exponent, axis=-1))
        softmax_weights = lax.optimization_barrier(exponent.astype(jnp.bfloat16)).astype(jnp.float32)
        weighted_values = jnp.einsum('bzv,bvn->bzn', softmax_weights, common_prefix[:, :, HEAD_SIZE:])
        old_max, old_tot, old_sum = running
        largest = jnp.maximum(old_max, maxima)
        keep_old = jnp.exp(old_max - largest)
        keep_new = jnp.exp(maxima - largest)
        return ((largest, old_tot * keep_old + totals * keep_new, old_sum * keep_old[..., None] + weighted_values * keep_new[..., None]), None)
    start = (jnp.full((KVH, REQUESTS * GROUP), -1e+30, jnp.float32), jnp.zeros((KVH, REQUESTS * GROUP), jnp.float32), jnp.zeros((KVH, REQUESTS * GROUP, HEAD_SIZE), jnp.float32))
    final, unused = lax.scan(visit, start, jnp.arange(N_BLK, dtype=jnp.int32))
    largest, norm, combined = final
    attended = (combined / norm[..., None]).astype(jnp.bfloat16)
    return attended.reshape(KVH, REQUESTS, GROUP, HEAD_SIZE).transpose(1, 0, 2, 3).reshape(REQUESTS, QH, HEAD_SIZE)
```

```python
import functools
import math

import jax
import jax.numpy as jnp
from jax import lax
from jax.experimental import pallas as pl
from jax.experimental.pallas import tpu as pltpu
from jax.sharding import PartitionSpec as P

MESH = pl.DeviceIdType.MESH
NZ, NX, NC = 8, 2, 2
NH, NY = 2, 4
POOL = NH * NY
BS, D = 16, 128
NB, CAP = 96, 24
ROWS = 128
SPLIT = (8, 8, 8)
PEERS = ((0, 1), (0, 3), (1, 0), (0, 2), (1, 1), (1, 3), (1, 2))
PAIR = 2 * NX * ROWS
TILES = NZ // 2
PACK = D + 16
SCALE = math.log2(math.e) / math.sqrt(D)
LOG2E = math.log2(math.e)


def slot_of(dz):
    return 0 if dz == 0 else (2 * dz - 1 if dz <= NZ // 2 else 2 * (NZ - dz))


def step_of(slot):
    return (slot + 1) // 2 if slot % 2 else (NZ - slot // 2) % NZ


def packing(owner_ref, table_ref):
    owner = owner_ref[...]
    counts = [jnp.sum((owner == j).astype(jnp.int32), axis=1, keepdims=True) for j in range(POOL)]
    place = lax.broadcasted_iota(jnp.int32, (1, 128), 1)
    source = place
    ahead = None
    start = 0
    for size in SPLIT:
        for j in range(POOL):
            here = jnp.clip(counts[j] - start, 0, size)
            ahead = here if ahead is None else ahead + here
            source = source + jnp.where(place >= ahead, size - here, 0)
        start += size
    table_ref[...] = jnp.where(place < NB, jnp.minimum(source, POOL * CAP - 1), 0)


def kernel(
    q_ref, kv_ref, owner_ref, o_ref,
    qbuf, arrived, staged, packed, table_v, table_s, vt, scores, acc, peak, total,
    xsend, xrecv, zsend, zrecv,
    kv_ssem, kv_rsem, own_sem, table_sem, qx_ssem, qx_rsem, qz_ssem, qz_rsem, c_ssem, c_rsem,
    xs_sem, xr_sem, zs_sem, zr_sem,
):
    blk, pool = lax.axis_index("blk"), lax.axis_index("pool")
    z, xl, core = blk // (NX * NC), (blk // NC) % NX, blk % NC
    xh, y = pool // NY, pool % NY

    def pool_peer(dx, dy):
        return (blk, ((xh + dx) % NH) * NY + (y + dy) % NY)

    def z_peer(dz):
        return (((z + dz) % NZ) * (NX * NC) + xl * NC + core, pool)

    x_peer = (z * (NX * NC) + (1 - xl) * NC + core, pool)
    core_peer = (z * (NX * NC) + xl * NC + (1 - core), pool)

    def remote(src, dst, ssem, rsem, device):
        return pltpu.make_async_remote_copy(
            src_ref=src, dst_ref=dst, send_sem=ssem, recv_sem=rsem, device_id=device, device_id_type=MESH
        )

    barrier = pltpu.get_barrier_semaphore()
    everyone = [z_peer(d) for d in range(1, NZ)] + [pool_peer(*p) for p in PEERS] + [x_peer, core_peer]
    for device in everyone:
        pl.semaphore_signal(barrier, inc=1, device_id=device, device_id_type=MESH)

    own = []
    start = 0
    for m, size in enumerate(SPLIT):
        copy = pltpu.make_async_copy(
            kv_ref.at[pool, pl.ds(start, size)], arrived.at[pl.ds(start * POOL + pool * size, size)], own_sem.at[m]
        )
        copy.start()
        own.append(copy)
        start += size
    qbuf[0, 0] = q_ref[...].reshape(ROWS, D)
    packing(owner_ref, table_v)
    to_smem = pltpu.make_async_copy(table_v, table_s, table_sem)
    to_smem.start()
    to_smem.wait()

    pl.semaphore_wait(barrier, len(everyone))

    qx = remote(qbuf.at[0, 0], qbuf.at[0, 1], qx_ssem, qx_rsem, x_peer)
    qx.start()
    qz = [None] * (2 * NZ)
    order = [step_of(s) for s in range(1, NZ)]
    for d in order:
        at = slot_of(NZ - d)
        qz[2 * at] = remote(qbuf.at[0, 0], qbuf.at[at, 0], qz_ssem.at[2 * at], qz_rsem.at[2 * at], z_peer(d))
        qz[2 * at].start()
    moves = []
    start = 0
    for m, size in enumerate(SPLIT):
        part = []
        for i, (dx, dy) in enumerate(PEERS):
            device = pool_peer(dx, dy)
            copy = remote(
                kv_ref.at[device[1], pl.ds(start, size)], arrived.at[pl.ds(start * POOL + pool * size, size)],
                kv_ssem.at[m, i], kv_rsem.at[m, i], device,
            )
            copy.start()
            part.append(copy)
        moves.append(part)
        start += size
        if m == 0:
            qx.wait_recv()
            for d in order:
                at = slot_of(NZ - d)
                qz[2 * at + 1] = remote(
                    qbuf.at[0, 1], qbuf.at[at, 1], qz_ssem.at[2 * at + 1], qz_rsem.at[2 * at + 1], z_peer(d)
                )
                qz[2 * at + 1].start()

    x_moves, z_moves = [None] * NZ, [None] * NZ

    def split3(v):
        high = v.astype(jnp.bfloat16)
        rest = v - high.astype(jnp.float32)
        mid = rest.astype(jnp.bfloat16)
        low = (rest - mid.astype(jnp.float32)).astype(jnp.bfloat16)
        return high, mid, low

    def put(ref, s, value, lse):
        ref[s, pl.ds(0, D)] = value.astype(jnp.bfloat16)
        parts = jnp.concatenate([p.astype(jnp.float32) for p in split3(lse)] + [jnp.zeros((13, ROWS), jnp.float32)], axis=0)
        ref[s, pl.ds(D, 16)] = parts.astype(jnp.bfloat16)

    def get(ref, s):
        tail = ref[s, pl.ds(D, 16)].astype(jnp.float32)
        return ref[s, pl.ds(0, D)].astype(jnp.float32), tail[0:1] + tail[1:2] + tail[2:3]

    def combine(s):
        x_moves[s].wait_recv()
        t, lanes = s // 2, pl.ds((s % 2) * NX * ROWS, ROWS)
        mine, lse_a = acc[t, :, lanes], peak[t, :, lanes]
        theirs, lse_b = get(xrecv, s)
        top = jnp.maximum(lse_a, lse_b)
        wa, wb = jnp.exp2(lse_a - top), jnp.exp2(lse_b - top)
        norm = wa + wb
        inv = 1.0 / norm
        put(zsend, s, mine * (wa * inv) + theirs * (wb * inv), top + jnp.log(norm) * LOG2E)
        if s > 0:
            z_moves[s] = remote(zsend.at[s], zrecv.at[s], zs_sem.at[s], zr_sem.at[s], z_peer(step_of(s)))
            z_moves[s].start()

    swaps = []
    start = 0
    last = len(SPLIT) - 1
    for m, size in enumerate(SPLIT):
        blocks = size * POOL // 2
        own[m].wait()
        for copy in moves[m]:
            copy.wait_recv()
        staged[pl.ds(start * POOL, size * POOL)] = arrived[pl.ds(start * POOL, size * POOL)]
        base = start * POOL
        for p in range(blocks):
            packed[base + p] = staged[table_s[0, start * POOL // 2 + p]]
        swap = remote(
            packed.at[pl.ds(base, blocks)], packed.at[pl.ds(base + blocks, blocks)], c_ssem.at[m], c_rsem.at[m], core_peer
        )
        swap.start()
        swaps.append(swap)
        swap.wait_recv()
        tokens = 2 * blocks * BS
        vt[m % 2, :, pl.ds(0, tokens)] = jnp.swapaxes(
            packed[pl.ds(base, 2 * blocks), :, D:].reshape(tokens, D), 0, 1
        )

        def score(t, b):
            if m == 0:
                for s in (2 * t, 2 * t + 1):
                    if s > 0:
                        qz[2 * s].wait_recv()
                        qz[2 * s + 1].wait_recv()
            keys = packed[pl.ds(base, 2 * blocks), :, :D].reshape(tokens, D)
            rows = qbuf[pl.ds(2 * t, 2)].reshape(PAIR, D)
            scores[b, pl.ds(0, tokens)] = lax.dot_general(
                keys, rows, (((1,), (1,)), ((), ())), preferred_element_type=jnp.float32
            )

        def soft(t, b):
            s = scores[b, pl.ds(0, tokens)]
            high = jnp.max(s, axis=0, keepdims=True)
            if m > 0:
                before = peak[t]
                high = jnp.maximum(high, before)
            high_c = high * SCALE
            weight = jnp.exp2(s * SCALE - high_c)
            mass = jnp.sum(weight, axis=0, keepdims=True)
            out = jnp.dot(vt[m % 2, :, pl.ds(0, tokens)], weight.astype(jnp.bfloat16), preferred_element_type=jnp.float32)
            if m > 0:
                keep = jnp.exp2(before * SCALE - high_c)
                mass = mass + keep * total[t]
                out = out + keep * acc[t]
            if m < last:
                peak[t] = high
                total[t] = mass
                acc[t] = out
                return
            out = out * (1.0 / mass)
            lse = high_c + jnp.log(mass) * LOG2E
            acc[t] = out
            peak[t] = lse
            for h in (1, 0):
                slot = 2 * t + h
                lanes = slice((2 * h + 1) * ROWS, (2 * h + 2) * ROWS)
                put(xsend, slot, out[:, lanes], lse[:, lanes])
                x_moves[slot] = remote(xsend.at[slot], xrecv.at[slot], xs_sem.at[slot], xr_sem.at[slot], x_peer)
                x_moves[slot].start()

        tiles = list(range(TILES))
        if m == last:
            tiles = tiles[::-1]
        score(tiles[0], 0)
        for i, t in enumerate(tiles):
            if i + 1 < TILES:
                score(tiles[i + 1], (i + 1) % 2)
            soft(t, i % 2)
            if m == last and i >= 1:
                combine(2 * tiles[i - 1] + 1)
                combine(2 * tiles[i - 1])
        start += size
    combine(1)
    combine(0)

    values, logs = [], []
    for s in range(NZ):
        if s > 0:
            z_moves[s].wait_recv()
        value, lse = get(zsend if s == 0 else zrecv, s)
        values.append(value)
        logs.append(lse)
    top = functools.reduce(jnp.maximum, logs)
    weights = [jnp.exp2(v - top) for v in logs]
    inv = 1.0 / functools.reduce(jnp.add, weights)
    result = functools.reduce(jnp.add, [v * (w * inv) for v, w in zip(values, weights)])
    o_ref[...] = jnp.swapaxes(result, 0, 1).astype(jnp.bfloat16).reshape(o_ref.shape)

    qx.wait_send()
    for copy in qz[2:]:
        copy.wait_send()
    for part in moves:
        for copy in part:
            copy.wait_send()
    for copy in swaps + x_moves + z_moves[1:]:
        copy.wait_send()


def body(queries, kv_cache, block_owner):
    widest = max(SPLIT) * POOL * BS
    dma = pltpu.SemaphoreType.DMA
    return pl.pallas_call(
        kernel,
        out_shape=jax.ShapeDtypeStruct(queries.shape, queries.dtype),
        in_specs=[
            pl.BlockSpec(memory_space=pltpu.VMEM),
            pl.BlockSpec(memory_space=pltpu.HBM),
            pl.BlockSpec(memory_space=pltpu.VMEM),
        ],
        out_specs=pl.BlockSpec(memory_space=pltpu.VMEM),
        scratch_shapes=[
            pltpu.VMEM((NZ, NX, ROWS, D), jnp.bfloat16),
            pltpu.VMEM((POOL * CAP, BS, 2 * D), jnp.bfloat16),
            pltpu.VMEM((POOL * CAP, BS, 2 * D), jnp.bfloat16),
            pltpu.VMEM((2 * NB, BS, 2 * D), jnp.bfloat16),
            pltpu.VMEM((1, 128), jnp.int32),
            pltpu.SMEM((1, 128), jnp.int32),
            pltpu.VMEM((2, D, widest), jnp.bfloat16),
            pltpu.VMEM((2, widest, PAIR), jnp.float32),
            pltpu.VMEM((TILES, D, PAIR), jnp.float32),
            pltpu.VMEM((TILES, 1, PAIR), jnp.float32),
            pltpu.VMEM((TILES, 1, PAIR), jnp.float32),
            pltpu.VMEM((NZ, PACK, ROWS), jnp.bfloat16),
            pltpu.VMEM((NZ, PACK, ROWS), jnp.bfloat16),
            pltpu.VMEM((NZ, PACK, ROWS), jnp.bfloat16),
            pltpu.VMEM((NZ, PACK, ROWS), jnp.bfloat16),
            dma((len(SPLIT), len(PEERS))),
            dma((len(SPLIT), len(PEERS))),
            dma((len(SPLIT),)),
            dma,
            dma,
            dma,
            dma((2 * NZ,)),
            dma((2 * NZ,)),
            dma((len(SPLIT),)),
            dma((len(SPLIT),)),
            dma((NZ,)),
            dma((NZ,)),
            dma((NZ,)),
            dma((NZ,)),
        ],
        compiler_params=pltpu.CompilerParams(
            collective_id=0, has_side_effects=True, vmem_limit_bytes=48 * 1024 * 1024
        ),
        cost_estimate=pl.CostEstimate(flops=3_300_000_000, bytes_accessed=4_000_000, transcendentals=6_300_000),
    )(queries, kv_cache, block_owner.reshape(1, NB))


def solution(mesh):
    in_specs = (P("blk", "pool", None), P(None, ("blk", "pool"), None, None), P("blk", None))
    out_specs = P("blk", "pool", None)
    return jax.shard_map(body, mesh=mesh, in_specs=in_specs, out_specs=out_specs, check_vma=False)
```

```python
import functools
import math

import jax
import jax.numpy as jnp
from jax import lax
from jax.experimental import pallas as pl
from jax.experimental.pallas import tpu as pltpu
from jax.sharding import PartitionSpec as P

MESH = pl.DeviceIdType.MESH
NZ, NX, NC = 8, 2, 2
NH, NY = 2, 4
POOL = NH * NY
BS, D = 16, 128
NB, CAP = 96, 24
REQ, HEADS = 8, 16
ROWS = REQ * HEADS
SPLIT = (8, 8, 8)
PEERS = ((1, 2), (1, 1), (1, 3), (1, 0), (0, 2), (0, 1), (0, 3))
PAIR = 2 * NX * ROWS
TILES = NZ // 2
PACK = D + 16
SCALE = math.log2(math.e) / math.sqrt(D)
LOG2E = math.log2(math.e)


def slot_of(dz):
    return 0 if dz == 0 else (2 * dz - 1 if dz <= NZ // 2 else 2 * (NZ - dz))


def step_of(slot):
    return (slot + 1) // 2 if slot % 2 else (NZ - slot // 2) % NZ


def packing(owner_ref, table_ref):
    owner = owner_ref[...]
    counts = [jnp.sum((owner == j).astype(jnp.int32), axis=1, keepdims=True) for j in range(POOL)]
    place = lax.broadcasted_iota(jnp.int32, (1, 128), 1)
    source = place
    ahead = None
    start = 0
    for size in SPLIT:
        for j in range(POOL):
            here = jnp.clip(counts[j] - start, 0, size)
            ahead = here if ahead is None else ahead + here
            source = source + jnp.where(place >= ahead, size - here, 0)
        start += size
    table_ref[...] = jnp.where(place < NB, jnp.minimum(source, POOL * CAP - 1), 0)


def kernel(
    q_ref, kv_ref, owner_ref, o_ref,
    owner_v, kv_v, qbuf, arrived, staged, packed, table_v, table_s, vt, scores, acc, peak, total,
    xsend, xrecv, zsend, zrecv,
    kv_ssem, kv_rsem, own_sem, first_sem, table_sem, qx_ssem, qx_rsem, qz_ssem, qz_rsem, c_ssem, c_rsem,
    xs_sem, xr_sem, zs_sem, zr_sem,
):
    blk, pool = lax.axis_index("blk"), lax.axis_index("pool")
    z, xl, core = blk // (NX * NC), (blk // NC) % NX, blk % NC
    xh, y = pool // NY, pool % NY

    def pool_peer(dx, dy):
        return (blk, ((xh + dx) % NH) * NY + (y + dy) % NY)

    def z_peer(dz):
        return (((z + dz) % NZ) * (NX * NC) + xl * NC + core, pool)

    x_peer = (z * (NX * NC) + (1 - xl) * NC + core, pool)
    core_peer = (z * (NX * NC) + xl * NC + (1 - core), pool)

    def remote(src, dst, ssem, rsem, device):
        return pltpu.make_async_remote_copy(
            src_ref=src, dst_ref=dst, send_sem=ssem, recv_sem=rsem, device_id=device, device_id_type=MESH
        )

    barrier = pltpu.get_barrier_semaphore()
    everyone = [z_peer(d) for d in range(1, NZ)] + [pool_peer(*p) for p in PEERS] + [x_peer, core_peer]
    for device in everyone:
        pl.semaphore_signal(barrier, inc=1, device_id=device, device_id_type=MESH)

    rows_in = pltpu.make_async_copy(q_ref, qbuf.at[0, 0], first_sem.at[0])
    rows_in.start()
    owners_in = pltpu.make_async_copy(owner_ref, owner_v, first_sem.at[1])
    owners_in.start()
    held = []
    start = 0
    for m, size in enumerate(SPLIT):
        copy = pltpu.make_async_copy(kv_ref.at[:, pl.ds(start, size)], kv_v.at[:, pl.ds(start, size)], own_sem.at[m])
        copy.start()
        held.append(copy)
        start += size
    rows_in.wait()
    pl.semaphore_wait(barrier, len(everyone))

    qx = remote(qbuf.at[0, 0], qbuf.at[0, 1], qx_ssem, qx_rsem, x_peer)
    qx.start()
    qz = [None] * (2 * NZ)
    order = [step_of(s) for s in range(1, NZ)]

    def send_rows(h):
        for d in order:
            at = slot_of(NZ - d)
            k = 2 * at + h
            qz[k] = remote(qbuf.at[0, h], qbuf.at[at, h], qz_ssem.at[k], qz_rsem.at[k], z_peer(d))
            qz[k].start()

    moves = []
    start = 0
    for m, size in enumerate(SPLIT):
        held[m].wait()
        part = []
        for i, (dx, dy) in enumerate(PEERS):
            device = pool_peer(dx, dy)
            copy = remote(
                kv_v.at[device[1], pl.ds(start, size)], arrived.at[pl.ds(start * POOL + pool * size, size)],
                kv_ssem.at[m, i], kv_rsem.at[m, i], device,
            )
            copy.start()
            part.append(copy)
        moves.append(part)
        start += size
        if m == 0:
            send_rows(0)
    qx.wait_recv()
    send_rows(1)
    owners_in.wait()
    packing(owner_v, table_v)
    to_smem = pltpu.make_async_copy(table_v, table_s, table_sem)
    to_smem.start()
    to_smem.wait()

    x_moves, z_moves = [None] * NZ, [None] * NZ

    def split3(v):
        high = v.astype(jnp.bfloat16)
        rest = v - high.astype(jnp.float32)
        mid = rest.astype(jnp.bfloat16)
        low = (rest - mid.astype(jnp.float32)).astype(jnp.bfloat16)
        return high, mid, low

    def put(ref, s, value, lse):
        ref[s, pl.ds(0, D)] = value.astype(jnp.bfloat16)
        parts = jnp.concatenate([p.astype(jnp.float32) for p in split3(lse)] + [jnp.zeros((13, ROWS), jnp.float32)], axis=0)
        ref[s, pl.ds(D, 16)] = parts.astype(jnp.bfloat16)

    def get(ref, s):
        tail = ref[s, pl.ds(D, 16)].astype(jnp.float32)
        return ref[s, pl.ds(0, D)].astype(jnp.float32), tail[0:1] + tail[1:2] + tail[2:3]

    def combine(s):
        x_moves[s].wait_recv()
        t, lanes = s // 2, pl.ds((s % 2) * NX * ROWS, ROWS)
        mine, lse_a = acc[t, :, lanes], peak[t, :, lanes]
        theirs, lse_b = get(xrecv, s)
        top = jnp.maximum(lse_a, lse_b)
        wa, wb = jnp.exp2(lse_a - top), jnp.exp2(lse_b - top)
        norm = wa + wb
        inv = 1.0 / norm
        put(zsend, s, mine * (wa * inv) + theirs * (wb * inv), top + jnp.log(norm) * LOG2E)
        if s > 0:
            z_moves[s] = remote(zsend.at[s], zrecv.at[s], zs_sem.at[s], zr_sem.at[s], z_peer(step_of(s)))
            z_moves[s].start()

    def attend(turn, base, blocks, final=False):
        first = turn == 0
        tokens = blocks * BS
        side = turn % 2
        vt[side, :, pl.ds(0, tokens)] = jnp.swapaxes(packed[pl.ds(base, blocks), :, D:].reshape(tokens, D), 0, 1)

        def score(t, b):
            if first:
                for s in (2 * t, 2 * t + 1):
                    if s > 0:
                        qz[2 * s].wait_recv()
                        qz[2 * s + 1].wait_recv()
            keys = packed[pl.ds(base, blocks), :, :D].reshape(tokens, D)
            rows = qbuf[pl.ds(2 * t, 2)].reshape(PAIR, D)
            scores[b, pl.ds(0, tokens)] = lax.dot_general(
                keys, rows, (((1,), (1,)), ((), ())), preferred_element_type=jnp.float32
            )

        def soft(t, b):
            s = scores[b, pl.ds(0, tokens)]
            high = jnp.max(s, axis=0, keepdims=True)
            if not first:
                previous = peak[t]
                high = jnp.maximum(high, previous)
            high_c = high * SCALE
            weight = jnp.exp2(s * SCALE - high_c)
            mass = jnp.sum(weight, axis=0, keepdims=True)
            out = jnp.dot(vt[side, :, pl.ds(0, tokens)], weight.astype(jnp.bfloat16), preferred_element_type=jnp.float32)
            if not first:
                keep = jnp.exp2(previous * SCALE - high_c)
                mass = mass + keep * total[t]
                out = out + keep * acc[t]
            if not final:
                peak[t] = high
                total[t] = mass
                acc[t] = out
                return
            out = out * (1.0 / mass)
            lse = high_c + jnp.log(mass) * LOG2E
            acc[t] = out
            peak[t] = lse
            for h in (1, 0):
                slot = 2 * t + h
                lanes = slice((2 * h + 1) * ROWS, (2 * h + 2) * ROWS)
                put(xsend, slot, out[:, lanes], lse[:, lanes])
                x_moves[slot] = remote(xsend.at[slot], xrecv.at[slot], xs_sem.at[slot], xr_sem.at[slot], x_peer)
                x_moves[slot].start()

        tiles = list(range(TILES))
        if final:
            tiles = tiles[::-1]
        score(tiles[0], 0)
        for i, t in enumerate(tiles):
            if i + 1 < TILES:
                score(tiles[i + 1], (i + 1) % 2)
            soft(t, i % 2)
            if final and i >= 1:
                combine(2 * tiles[i - 1] + 1)
                combine(2 * tiles[i - 1])

    swaps = []
    start = 0
    for m, size in enumerate(SPLIT):
        blocks = size * POOL // 2
        for copy in moves[m]:
            copy.wait_recv()
        staged[pl.ds(start * POOL, size * POOL)] = arrived[pl.ds(start * POOL, size * POOL)]
        staged[pl.ds(start * POOL + pool * size, size)] = kv_v[pool, pl.ds(start, size)]
        base = start * POOL
        for p in range(blocks):
            packed[base + p] = staged[table_s[0, start * POOL // 2 + p]]
        swap = remote(
            packed.at[pl.ds(base, blocks)], packed.at[pl.ds(base + blocks, blocks)], c_ssem.at[m], c_rsem.at[m], core_peer
        )
        swap.start()
        swaps.append(swap)
        if m == 0:
            attend(0, 0, blocks)
        else:
            swaps[m - 1].wait_recv()
            attend(m, base - before, before + blocks)
        before = blocks
        start += size
    swaps[-1].wait_recv()
    attend(len(SPLIT), base + blocks, blocks, final=True)
    combine(1)
    combine(0)

    values, logs = [], []
    for s in range(NZ):
        if s > 0:
            z_moves[s].wait_recv()
        value, lse = get(zsend if s == 0 else zrecv, s)
        values.append(value)
        logs.append(lse)
    top = functools.reduce(jnp.maximum, logs)
    weights = [jnp.exp2(v - top) for v in logs]
    inv = 1.0 / functools.reduce(jnp.add, weights)
    result = functools.reduce(jnp.add, [v * (w * inv) for v, w in zip(values, weights)])
    o_ref[...] = jnp.swapaxes(result, 0, 1).astype(jnp.bfloat16).reshape(o_ref.shape)

    qx.wait_send()
    for copy in qz[2:]:
        copy.wait_send()
    for part in moves:
        for copy in part:
            copy.wait_send()
    for copy in swaps + x_moves + z_moves[1:]:
        copy.wait_send()


def body(queries, kv_cache, block_owner):
    widest = max(a + b for a, b in zip(SPLIT, SPLIT[1:])) * POOL // 2 * BS
    dma = pltpu.SemaphoreType.DMA
    return pl.pallas_call(
        kernel,
        out_shape=jax.ShapeDtypeStruct(queries.shape, queries.dtype),
        in_specs=[
            pl.BlockSpec(memory_space=pltpu.HBM),
            pl.BlockSpec(memory_space=pltpu.HBM),
            pl.BlockSpec(memory_space=pltpu.HBM),
        ],
        out_specs=pl.BlockSpec(memory_space=pltpu.VMEM),
        scratch_shapes=[
            pltpu.VMEM((1, NB), jnp.int32),
            pltpu.VMEM((POOL, CAP, BS, 2 * D), jnp.bfloat16),
            pltpu.VMEM((NZ, NX, REQ, HEADS, D), jnp.bfloat16),
            pltpu.VMEM((POOL * CAP, BS, 2 * D), jnp.bfloat16),
            pltpu.VMEM((POOL * CAP, BS, 2 * D), jnp.bfloat16),
            pltpu.VMEM((2 * NB, BS, 2 * D), jnp.bfloat16),
            pltpu.VMEM((1, 128), jnp.int32),
            pltpu.SMEM((1, 128), jnp.int32),
            pltpu.VMEM((2, D, widest), jnp.bfloat16),
            pltpu.VMEM((2, widest, PAIR), jnp.float32),
            pltpu.VMEM((TILES, D, PAIR), jnp.float32),
            pltpu.VMEM((TILES, 1, PAIR), jnp.float32),
            pltpu.VMEM((TILES, 1, PAIR), jnp.float32),
            pltpu.VMEM((NZ, PACK, ROWS), jnp.bfloat16),
            pltpu.VMEM((NZ, PACK, ROWS), jnp.bfloat16),
            pltpu.VMEM((NZ, PACK, ROWS), jnp.bfloat16),
            pltpu.VMEM((NZ, PACK, ROWS), jnp.bfloat16),
            dma((len(SPLIT), len(PEERS))),
            dma((len(SPLIT), len(PEERS))),
            dma((len(SPLIT),)),
            dma((2,)),
            dma,
            dma,
            dma,
            dma((2 * NZ,)),
            dma((2 * NZ,)),
            dma((len(SPLIT),)),
            dma((len(SPLIT),)),
            dma((NZ,)),
            dma((NZ,)),
            dma((NZ,)),
            dma((NZ,)),
        ],
        compiler_params=pltpu.CompilerParams(
            collective_id=0, has_side_effects=True, vmem_limit_bytes=63 * 1024 * 1024
        ),
        cost_estimate=pl.CostEstimate(flops=3_300_000_000, bytes_accessed=4_000_000, transcendentals=6_300_000),
    )(queries, kv_cache, block_owner.reshape(1, NB))


def solution(mesh):
    in_specs = (P("blk", "pool", None), P(None, ("blk", "pool"), None, None), P("blk", None))
    out_specs = P("blk", "pool", None)
    return jax.shard_map(body, mesh=mesh, in_specs=in_specs, out_specs=out_specs, check_vma=False)
```

```python
import functools
import math

import jax
import jax.numpy as jnp
from jax import lax
from jax.experimental import pallas as pl
from jax.experimental.pallas import tpu as pltpu
from jax.sharding import PartitionSpec as P

MESH = pl.DeviceIdType.MESH
NZ, NX, NC = 8, 2, 2
NH, NY = 2, 4
POOL = NH * NY
BS, D = 16, 128
NB, CAP = 96, 24
REQ, HEADS = 8, 16
ROWS = REQ * HEADS
SPLIT = (8, 8, 8)
PEERS = ((1, 2), (1, 1), (1, 3), (1, 0), (0, 2), (0, 1), (0, 3))
PAIR = 2 * NX * ROWS
TILES = NZ // 2
PACK = D + 16
SCALE = math.log2(math.e) / math.sqrt(D)
LOG2E = math.log2(math.e)


def slot_of(dz):
    return 0 if dz == 0 else (2 * dz - 1 if dz <= NZ // 2 else 2 * (NZ - dz))


def step_of(slot):
    return (slot + 1) // 2 if slot % 2 else (NZ - slot // 2) % NZ


def packing(owner_ref, table_ref):
    owner = owner_ref[...]
    counts = [jnp.sum((owner == j).astype(jnp.int32), axis=1, keepdims=True) for j in range(POOL)]
    place = lax.broadcasted_iota(jnp.int32, (1, 128), 1)
    source = place
    ahead = None
    start = 0
    for size in SPLIT:
        for j in range(POOL):
            here = jnp.clip(counts[j] - start, 0, size)
            ahead = here if ahead is None else ahead + here
            source = source + jnp.where(place >= ahead, size - here, 0)
        start += size
    table_ref[...] = jnp.where(place < NB, jnp.minimum(source, POOL * CAP - 1), 0)


def kernel(
    q_ref, kv_ref, owner_ref, o_ref,
    owner_v, kv_v, qbuf, arrived, staged, packed, table_v, table_s, vt, scores, acc, peak, total,
    xsend, xrecv, zsend, zrecv,
    kv_ssem, kv_rsem, own_sem, first_sem, table_sem, qx_ssem, qx_rsem, qz_ssem, qz_rsem, c_ssem, c_rsem,
    xs_sem, xr_sem, zs_sem, zr_sem,
):
    blk, pool = lax.axis_index("blk"), lax.axis_index("pool")
    z, xl, core = blk // (NX * NC), (blk // NC) % NX, blk % NC
    xh, y = pool // NY, pool % NY

    def pool_peer(dx, dy):
        return (blk, ((xh + dx) % NH) * NY + (y + dy) % NY)

    def z_peer(dz):
        return (((z + dz) % NZ) * (NX * NC) + xl * NC + core, pool)

    x_peer = (z * (NX * NC) + (1 - xl) * NC + core, pool)
    core_peer = (z * (NX * NC) + xl * NC + (1 - core), pool)

    def remote(src, dst, ssem, rsem, device):
        return pltpu.make_async_remote_copy(
            src_ref=src, dst_ref=dst, send_sem=ssem, recv_sem=rsem, device_id=device, device_id_type=MESH
        )

    barrier = pltpu.get_barrier_semaphore()
    everyone = [z_peer(d) for d in range(1, NZ)] + [pool_peer(*p) for p in PEERS] + [x_peer, core_peer]
    for device in everyone:
        pl.semaphore_signal(barrier, inc=1, device_id=device, device_id_type=MESH)

    rows_in = pltpu.make_async_copy(q_ref, qbuf.at[0, 0], first_sem.at[0])
    rows_in.start()
    owners_in = pltpu.make_async_copy(owner_ref, owner_v, first_sem.at[1])
    owners_in.start()
    held = []
    start = 0
    for m, size in enumerate(SPLIT):
        copy = pltpu.make_async_copy(kv_ref.at[:, pl.ds(start, size)], kv_v.at[:, pl.ds(start, size)], own_sem.at[m])
        copy.start()
        held.append(copy)
        start += size
    rows_in.wait()
    pl.semaphore_wait(barrier, len(everyone))

    qx = remote(qbuf.at[0, 0], qbuf.at[0, 1], qx_ssem, qx_rsem, x_peer)
    qx.start()
    qz = [None] * (2 * NZ)
    order = [step_of(s) for s in range(1, NZ)]

    def send_rows(h):
        for d in order:
            at = slot_of(NZ - d)
            k = 2 * at + h
            qz[k] = remote(qbuf.at[0, h], qbuf.at[at, h], qz_ssem.at[k], qz_rsem.at[k], z_peer(d))
            qz[k].start()

    moves = []
    start = 0
    for m, size in enumerate(SPLIT):
        held[m].wait()
        part = []
        for i, (dx, dy) in enumerate(PEERS):
            device = pool_peer(dx, dy)
            copy = remote(
                kv_v.at[device[1], pl.ds(start, size)], arrived.at[pl.ds(start * POOL + pool * size, size)],
                kv_ssem.at[m, i], kv_rsem.at[m, i], device,
            )
            copy.start()
            part.append(copy)
        moves.append(part)
        start += size
        if m == 0:
            send_rows(0)
            qx.wait_recv()
            send_rows(1)
    owners_in.wait()
    packing(owner_v, table_v)
    to_smem = pltpu.make_async_copy(table_v, table_s, table_sem)
    to_smem.start()
    to_smem.wait()

    x_moves, z_moves = [None] * NZ, [None] * NZ

    def split3(v):
        high = v.astype(jnp.bfloat16)
        rest = v - high.astype(jnp.float32)
        mid = rest.astype(jnp.bfloat16)
        low = (rest - mid.astype(jnp.float32)).astype(jnp.bfloat16)
        return high, mid, low

    def put(ref, s, value, lse):
        ref[s, pl.ds(0, D)] = value.astype(jnp.bfloat16)
        parts = jnp.concatenate([p.astype(jnp.float32) for p in split3(lse)] + [jnp.zeros((13, ROWS), jnp.float32)], axis=0)
        ref[s, pl.ds(D, 16)] = parts.astype(jnp.bfloat16)

    def get(ref, s):
        tail = ref[s, pl.ds(D, 16)].astype(jnp.float32)
        return ref[s, pl.ds(0, D)].astype(jnp.float32), tail[0:1] + tail[1:2] + tail[2:3]

    def combine(s):
        x_moves[s].wait_recv()
        t, lanes = s // 2, pl.ds((s % 2) * NX * ROWS, ROWS)
        mine, lse_a = acc[t, :, lanes], peak[t, :, lanes]
        theirs, lse_b = get(xrecv, s)
        top = jnp.maximum(lse_a, lse_b)
        wa, wb = jnp.exp2(lse_a - top), jnp.exp2(lse_b - top)
        norm = wa + wb
        inv = 1.0 / norm
        put(zsend, s, mine * (wa * inv) + theirs * (wb * inv), top + jnp.log(norm) * LOG2E)
        if s > 0:
            z_moves[s] = remote(zsend.at[s], zrecv.at[s], zs_sem.at[s], zr_sem.at[s], z_peer(step_of(s)))
            z_moves[s].start()

    def attend(turn, base, blocks, final=False):
        first = turn == 0
        tokens = blocks * BS
        side = turn % 2
        vt[side, :, pl.ds(0, tokens)] = jnp.swapaxes(packed[pl.ds(base, blocks), :, D:].reshape(tokens, D), 0, 1)

        def score(t, b):
            if first:
                for s in (2 * t, 2 * t + 1):
                    if s > 0:
                        qz[2 * s].wait_recv()
                        qz[2 * s + 1].wait_recv()
            keys = packed[pl.ds(base, blocks), :, :D].reshape(tokens, D)
            rows = qbuf[pl.ds(2 * t, 2)].reshape(PAIR, D)
            scores[b, pl.ds(0, tokens)] = lax.dot_general(
                keys, rows, (((1,), (1,)), ((), ())), preferred_element_type=jnp.float32
            )

        def soft(t, b):
            s = scores[b, pl.ds(0, tokens)]
            high = jnp.max(s, axis=0, keepdims=True)
            if not first:
                previous = peak[t]
                high = jnp.maximum(high, previous)
            high_c = high * SCALE
            weight = jnp.exp2(s * SCALE - high_c)
            mass = jnp.sum(weight, axis=0, keepdims=True)
            out = jnp.dot(vt[side, :, pl.ds(0, tokens)], weight.astype(jnp.bfloat16), preferred_element_type=jnp.float32)
            if not first:
                keep = jnp.exp2(previous * SCALE - high_c)
                mass = mass + keep * total[t]
                out = out + keep * acc[t]
            if not final:
                peak[t] = high
                total[t] = mass
                acc[t] = out
                return
            out = out * (1.0 / mass)
            lse = high_c + jnp.log(mass) * LOG2E
            acc[t] = out
            peak[t] = lse
            for h in (1, 0):
                slot = 2 * t + h
                lanes = slice((2 * h + 1) * ROWS, (2 * h + 2) * ROWS)
                put(xsend, slot, out[:, lanes], lse[:, lanes])
                x_moves[slot] = remote(xsend.at[slot], xrecv.at[slot], xs_sem.at[slot], xr_sem.at[slot], x_peer)
                x_moves[slot].start()

        tiles = list(range(TILES))
        if final:
            tiles = tiles[::-1]
        score(tiles[0], 0)
        for i, t in enumerate(tiles):
            if i + 1 < TILES:
                score(tiles[i + 1], (i + 1) % 2)
            soft(t, i % 2)
            if final and i >= 1:
                combine(2 * tiles[i - 1] + 1)
                combine(2 * tiles[i - 1])

    swaps = []
    start = 0
    for m, size in enumerate(SPLIT):
        blocks = size * POOL // 2
        for copy in moves[m]:
            copy.wait_recv()
        staged[pl.ds(start * POOL, size * POOL)] = arrived[pl.ds(start * POOL, size * POOL)]
        staged[pl.ds(start * POOL + pool * size, size)] = kv_v[pool, pl.ds(start, size)]
        base = start * POOL
        for p in range(blocks):
            packed[base + p] = staged[table_s[0, start * POOL // 2 + p]]
        swap = remote(
            packed.at[pl.ds(base, blocks)], packed.at[pl.ds(base + blocks, blocks)], c_ssem.at[m], c_rsem.at[m], core_peer
        )
        swap.start()
        swaps.append(swap)
        if m == 0:
            attend(0, 0, blocks)
        else:
            swaps[m - 1].wait_recv()
            attend(m, base - before, before + blocks)
        before = blocks
        start += size
    swaps[-1].wait_recv()
    attend(len(SPLIT), base + blocks, blocks, final=True)
    combine(1)
    combine(0)

    values, logs = [], []
    for s in range(NZ):
        if s > 0:
            z_moves[s].wait_recv()
        value, lse = get(zsend if s == 0 else zrecv, s)
        values.append(value)
        logs.append(lse)
    top = functools.reduce(jnp.maximum, logs)
    weights = [jnp.exp2(v - top) for v in logs]
    inv = 1.0 / functools.reduce(jnp.add, weights)
    result = functools.reduce(jnp.add, [v * (w * inv) for v, w in zip(values, weights)])
    o_ref[...] = jnp.swapaxes(result, 0, 1).astype(jnp.bfloat16).reshape(o_ref.shape)

    qx.wait_send()
    for copy in qz[2:]:
        copy.wait_send()
    for part in moves:
        for copy in part:
            copy.wait_send()
    for copy in swaps + x_moves + z_moves[1:]:
        copy.wait_send()


def body(queries, kv_cache, block_owner):
    widest = max(a + b for a, b in zip(SPLIT, SPLIT[1:])) * POOL // 2 * BS
    dma = pltpu.SemaphoreType.DMA
    return pl.pallas_call(
        kernel,
        out_shape=pltpu.VMEM(queries.shape, queries.dtype),
        in_specs=[
            pl.BlockSpec(memory_space=pltpu.HBM),
            pl.BlockSpec(memory_space=pltpu.HBM),
            pl.BlockSpec(memory_space=pltpu.HBM),
        ],
        out_specs=pl.BlockSpec(memory_space=pltpu.VMEM),
        scratch_shapes=[
            pltpu.VMEM((1, NB), jnp.int32),
            pltpu.VMEM((POOL, CAP, BS, 2 * D), jnp.bfloat16),
            pltpu.VMEM((NZ, NX, REQ, HEADS, D), jnp.bfloat16),
            pltpu.VMEM((POOL * CAP, BS, 2 * D), jnp.bfloat16),
            pltpu.VMEM((POOL * CAP, BS, 2 * D), jnp.bfloat16),
            pltpu.VMEM((2 * NB, BS, 2 * D), jnp.bfloat16),
            pltpu.VMEM((1, 128), jnp.int32),
            pltpu.SMEM((1, 128), jnp.int32),
            pltpu.VMEM((2, D, widest), jnp.bfloat16),
            pltpu.VMEM((2, widest, PAIR), jnp.float32),
            pltpu.VMEM((TILES, D, PAIR), jnp.float32),
            pltpu.VMEM((TILES, 1, PAIR), jnp.float32),
            pltpu.VMEM((TILES, 1, PAIR), jnp.float32),
            pltpu.VMEM((NZ, PACK, ROWS), jnp.bfloat16),
            pltpu.VMEM((NZ, PACK, ROWS), jnp.bfloat16),
            pltpu.VMEM((NZ, PACK, ROWS), jnp.bfloat16),
            pltpu.VMEM((NZ, PACK, ROWS), jnp.bfloat16),
            dma((len(SPLIT), len(PEERS))),
            dma((len(SPLIT), len(PEERS))),
            dma((len(SPLIT),)),
            dma((2,)),
            dma,
            dma,
            dma,
            dma((2 * NZ,)),
            dma((2 * NZ,)),
            dma((len(SPLIT),)),
            dma((len(SPLIT),)),
            dma((NZ,)),
            dma((NZ,)),
            dma((NZ,)),
            dma((NZ,)),
        ],
        compiler_params=pltpu.CompilerParams(
            collective_id=0, has_side_effects=True, vmem_limit_bytes=56 * 1024 * 1024
        ),
        cost_estimate=pl.CostEstimate(flops=3_300_000_000, bytes_accessed=4_000_000, transcendentals=6_300_000),
    )(queries, kv_cache, block_owner.reshape(1, NB))


def solution(mesh):
    in_specs = (P("blk", "pool", None), P(None, ("blk", "pool"), None, None), P("blk", None))
    out_specs = P("blk", "pool", None)
    return jax.shard_map(body, mesh=mesh, in_specs=in_specs, out_specs=out_specs, check_vma=False)
```

```python
import functools
import math

import jax
import jax.numpy as jnp
from jax import lax
from jax.experimental import pallas as pl
from jax.experimental.pallas import tpu as pltpu
from jax.sharding import PartitionSpec as P

MESH = pl.DeviceIdType.MESH
NZ, NX, NC = 8, 2, 2
NH, NY = 2, 4
POOL = NH * NY
BS, D = 16, 128
NB, CAP = 96, 24
REQ, HEADS = 8, 16
ROWS = REQ * HEADS
SPLIT = (8, 8, 8)
PEERS = ((1, 2), (1, 1), (1, 3), (1, 0), (0, 2), (0, 1), (0, 3))
PAIR = 2 * NX * ROWS
TILES = NZ // 2
PACK = D + 16
SCALE = math.log2(math.e) / math.sqrt(D)
LOG2E = math.log2(math.e)


def slot_of(dz):
    return 0 if dz == 0 else (2 * dz - 1 if dz <= NZ // 2 else 2 * (NZ - dz))


def step_of(slot):
    return (slot + 1) // 2 if slot % 2 else (NZ - slot // 2) % NZ


def packing(owner_ref, table_ref):
    owner = owner_ref[...]
    counts = [jnp.sum((owner == j).astype(jnp.int32), axis=1, keepdims=True) for j in range(POOL)]
    place = lax.broadcasted_iota(jnp.int32, (1, 128), 1)
    source = place
    ahead = None
    start = 0
    for size in SPLIT:
        for j in range(POOL):
            here = jnp.clip(counts[j] - start, 0, size)
            ahead = here if ahead is None else ahead + here
            source = source + jnp.where(place >= ahead, size - here, 0)
        start += size
    table_ref[...] = jnp.where(place < NB, jnp.minimum(source, POOL * CAP - 1), 0)


def kernel(
    q_ref, kv_ref, owner_ref, o_ref,
    owner_v, kv_v, qbuf, arrived, staged, packed, table_v, table_s, vt, scores, acc, peak, total,
    xsend, xrecv, zsend, zrecv,
    kv_ssem, kv_rsem, own_sem, first_sem, table_sem, qx_ssem, qx_rsem, qz_ssem, qz_rsem, c_ssem, c_rsem,
    xs_sem, xr_sem, zs_sem, zr_sem,
):
    blk, pool = lax.axis_index("blk"), lax.axis_index("pool")
    z, xl, core = blk // (NX * NC), (blk // NC) % NX, blk % NC
    xh, y = pool // NY, pool % NY

    def pool_peer(dx, dy):
        return (blk, ((xh + dx) % NH) * NY + (y + dy) % NY)

    def z_peer(dz):
        return (((z + dz) % NZ) * (NX * NC) + xl * NC + core, pool)

    x_peer = (z * (NX * NC) + (1 - xl) * NC + core, pool)
    core_peer = (z * (NX * NC) + xl * NC + (1 - core), pool)

    def remote(src, dst, ssem, rsem, device):
        return pltpu.make_async_remote_copy(
            src_ref=src, dst_ref=dst, send_sem=ssem, recv_sem=rsem, device_id=device, device_id_type=MESH
        )

    barrier = pltpu.get_barrier_semaphore()
    everyone = [z_peer(d) for d in range(1, NZ)] + [pool_peer(*p) for p in PEERS] + [x_peer, core_peer]
    for device in everyone:
        pl.semaphore_signal(barrier, inc=1, device_id=device, device_id_type=MESH)

    rows_in = pltpu.make_async_copy(q_ref, qbuf.at[0, 0], first_sem.at[0])
    rows_in.start()
    owners_in = pltpu.make_async_copy(owner_ref, owner_v, first_sem.at[1])
    owners_in.start()
    held = []
    start = 0
    for m, size in enumerate(SPLIT):
        copy = pltpu.make_async_copy(kv_ref.at[:, pl.ds(start, size)], kv_v.at[:, pl.ds(start, size)], own_sem.at[m])
        copy.start()
        held.append(copy)
        start += size
    rows_in.wait()
    pl.semaphore_wait(barrier, len(everyone))

    qx = remote(qbuf.at[0, 0], qbuf.at[0, 1], qx_ssem, qx_rsem, x_peer)
    qx.start()
    qz = [None] * (2 * NZ)
    order = [step_of(s) for s in range(1, NZ)]

    def send_rows(h):
        for d in order:
            at = slot_of(NZ - d)
            k = 2 * at + h
            qz[k] = remote(qbuf.at[0, h], qbuf.at[at, h], qz_ssem.at[k], qz_rsem.at[k], z_peer(d))
            qz[k].start()

    moves = []
    start = 0
    for m, size in enumerate(SPLIT):
        held[m].wait()
        part = []
        for i, (dx, dy) in enumerate(PEERS):
            device = pool_peer(dx, dy)
            copy = remote(
                kv_v.at[device[1], pl.ds(start, size)], arrived.at[pl.ds(start * POOL + pool * size, size)],
                kv_ssem.at[m, i], kv_rsem.at[m, i], device,
            )
            copy.start()
            part.append(copy)
        moves.append(part)
        start += size
        if m == 0:
            send_rows(0)
            qx.wait_recv()
            send_rows(1)
    owners_in.wait()
    packing(owner_v, table_v)
    to_smem = pltpu.make_async_copy(table_v, table_s, table_sem)
    to_smem.start()
    to_smem.wait()

    x_moves, z_moves = [None] * NZ, [None] * NZ

    def split3(v):
        high = v.astype(jnp.bfloat16)
        rest = v - high.astype(jnp.float32)
        mid = rest.astype(jnp.bfloat16)
        low = (rest - mid.astype(jnp.float32)).astype(jnp.bfloat16)
        return high, mid, low

    def put(ref, s, value, lse):
        ref[s, pl.ds(0, D)] = value.astype(jnp.bfloat16)
        parts = jnp.concatenate([p.astype(jnp.float32) for p in split3(lse)] + [jnp.zeros((13, ROWS), jnp.float32)], axis=0)
        ref[s, pl.ds(D, 16)] = parts.astype(jnp.bfloat16)

    def get(ref, s):
        tail = ref[s, pl.ds(D, 16)].astype(jnp.float32)
        return ref[s, pl.ds(0, D)].astype(jnp.float32), tail[0:1] + tail[1:2] + tail[2:3]

    def combine(s):
        x_moves[s].wait_recv()
        t, lanes = s // 2, pl.ds((s % 2) * NX * ROWS, ROWS)
        mine, lse_a = acc[t, :, lanes], peak[t, :, lanes]
        theirs, lse_b = get(xrecv, s)
        top = jnp.maximum(lse_a, lse_b)
        wa, wb = jnp.exp2(lse_a - top), jnp.exp2(lse_b - top)
        norm = wa + wb
        inv = 1.0 / norm
        put(zsend, s, mine * (wa * inv) + theirs * (wb * inv), top + jnp.log(norm) * LOG2E)
        if s > 0:
            z_moves[s] = remote(zsend.at[s], zrecv.at[s], zs_sem.at[s], zr_sem.at[s], z_peer(step_of(s)))
            z_moves[s].start()

    def attend(turn, base, blocks, final=False):
        first = turn == 0
        tokens = blocks * BS
        side = turn % 2
        vt[side, :, pl.ds(0, tokens)] = jnp.swapaxes(packed[pl.ds(base, blocks), :, D:].reshape(tokens, D), 0, 1)

        def score(t, b):
            if first:
                for s in (2 * t, 2 * t + 1):
                    if s > 0:
                        qz[2 * s].wait_recv()
                        qz[2 * s + 1].wait_recv()
            keys = packed[pl.ds(base, blocks), :, :D].reshape(tokens, D)
            rows = qbuf[pl.ds(2 * t, 2)].reshape(PAIR, D)
            scores[b, pl.ds(0, tokens)] = lax.dot_general(
                keys, rows, (((1,), (1,)), ((), ())), preferred_element_type=jnp.float32
            )

        def soft(t, b):
            s = scores[b, pl.ds(0, tokens)]
            high = jnp.max(s, axis=0, keepdims=True)
            if not first:
                previous = peak[t]
                high = jnp.maximum(high, previous)
            high_c = high * SCALE
            weight = jnp.exp2(s * SCALE - high_c)
            mass = jnp.sum(weight, axis=0, keepdims=True)
            out = jnp.dot(vt[side, :, pl.ds(0, tokens)], weight.astype(jnp.bfloat16), preferred_element_type=jnp.float32)
            if not first:
                keep = jnp.exp2(previous * SCALE - high_c)
                mass = mass + keep * total[t]
                out = out + keep * acc[t]
            if not final:
                peak[t] = high
                total[t] = mass
                acc[t] = out
                return
            out = out * (1.0 / mass)
            lse = high_c + jnp.log(mass) * LOG2E
            acc[t] = out
            peak[t] = lse
            for h in (1, 0):
                slot = 2 * t + h
                lanes = slice((2 * h + 1) * ROWS, (2 * h + 2) * ROWS)
                put(xsend, slot, out[:, lanes], lse[:, lanes])
                x_moves[slot] = remote(xsend.at[slot], xrecv.at[slot], xs_sem.at[slot], xr_sem.at[slot], x_peer)
                x_moves[slot].start()

        tiles = list(range(TILES))
        if final:
            tiles = tiles[::-1]
        score(tiles[0], 0)
        for i, t in enumerate(tiles):
            if i + 1 < TILES:
                score(tiles[i + 1], (i + 1) % 2)
            soft(t, i % 2)

    swaps = []
    start = 0
    for m, size in enumerate(SPLIT):
        blocks = size * POOL // 2
        for copy in moves[m]:
            copy.wait_recv()
        staged[pl.ds(start * POOL, size * POOL)] = arrived[pl.ds(start * POOL, size * POOL)]
        staged[pl.ds(start * POOL + pool * size, size)] = kv_v[pool, pl.ds(start, size)]
        base = start * POOL
        for p in range(blocks):
            packed[base + p] = staged[table_s[0, start * POOL // 2 + p]]
        swap = remote(
            packed.at[pl.ds(base, blocks)], packed.at[pl.ds(base + blocks, blocks)], c_ssem.at[m], c_rsem.at[m], core_peer
        )
        swap.start()
        swaps.append(swap)
        if m == 0:
            attend(0, 0, blocks)
        else:
            swaps[m - 1].wait_recv()
            attend(m, base - before, before + blocks)
        before = blocks
        start += size
    swaps[-1].wait_recv()
    attend(len(SPLIT), base + blocks, blocks, final=True)
    for s in range(NZ - 1, -1, -1):
        combine(s)

    values, logs = [], []
    for s in range(NZ):
        if s > 0:
            z_moves[s].wait_recv()
        value, lse = get(zsend if s == 0 else zrecv, s)
        values.append(value)
        logs.append(lse)
    top = functools.reduce(jnp.maximum, logs)
    weights = [jnp.exp2(v - top) for v in logs]
    inv = 1.0 / functools.reduce(jnp.add, weights)
    result = functools.reduce(jnp.add, [v * (w * inv) for v, w in zip(values, weights)])
    o_ref[...] = jnp.swapaxes(result, 0, 1).astype(jnp.bfloat16).reshape(o_ref.shape)

    qx.wait_send()
    for copy in qz[2:]:
        copy.wait_send()
    for part in moves:
        for copy in part:
            copy.wait_send()
    for copy in swaps + x_moves + z_moves[1:]:
        copy.wait_send()


def body(queries, kv_cache, block_owner):
    widest = max(a + b for a, b in zip(SPLIT, SPLIT[1:])) * POOL // 2 * BS
    dma = pltpu.SemaphoreType.DMA
    return pl.pallas_call(
        kernel,
        out_shape=pltpu.VMEM(queries.shape, queries.dtype),
        in_specs=[
            pl.BlockSpec(memory_space=pltpu.HBM),
            pl.BlockSpec(memory_space=pltpu.HBM),
            pl.BlockSpec(memory_space=pltpu.HBM),
        ],
        out_specs=pl.BlockSpec(memory_space=pltpu.VMEM),
        scratch_shapes=[
            pltpu.VMEM((1, NB), jnp.int32),
            pltpu.VMEM((POOL, CAP, BS, 2 * D), jnp.bfloat16),
            pltpu.VMEM((NZ, NX, REQ, HEADS, D), jnp.bfloat16),
            pltpu.VMEM((POOL * CAP, BS, 2 * D), jnp.bfloat16),
            pltpu.VMEM((POOL * CAP, BS, 2 * D), jnp.bfloat16),
            pltpu.VMEM((2 * NB, BS, 2 * D), jnp.bfloat16),
            pltpu.VMEM((1, 128), jnp.int32),
            pltpu.SMEM((1, 128), jnp.int32),
            pltpu.VMEM((2, D, widest), jnp.bfloat16),
            pltpu.VMEM((2, widest, PAIR), jnp.float32),
            pltpu.VMEM((TILES, D, PAIR), jnp.float32),
            pltpu.VMEM((TILES, 1, PAIR), jnp.float32),
            pltpu.VMEM((TILES, 1, PAIR), jnp.float32),
            pltpu.VMEM((NZ, PACK, ROWS), jnp.bfloat16),
            pltpu.VMEM((NZ, PACK, ROWS), jnp.bfloat16),
            pltpu.VMEM((NZ, PACK, ROWS), jnp.bfloat16),
            pltpu.VMEM((NZ, PACK, ROWS), jnp.bfloat16),
            dma((len(SPLIT), len(PEERS))),
            dma((len(SPLIT), len(PEERS))),
            dma((len(SPLIT),)),
            dma((2,)),
            dma,
            dma,
            dma,
            dma((2 * NZ,)),
            dma((2 * NZ,)),
            dma((len(SPLIT),)),
            dma((len(SPLIT),)),
            dma((NZ,)),
            dma((NZ,)),
            dma((NZ,)),
            dma((NZ,)),
        ],
        compiler_params=pltpu.CompilerParams(
            collective_id=0, has_side_effects=True, vmem_limit_bytes=56 * 1024 * 1024
        ),
        cost_estimate=pl.CostEstimate(flops=3_300_000_000, bytes_accessed=4_000_000, transcendentals=6_300_000),
    )(queries, kv_cache, block_owner.reshape(1, NB))


def solution(mesh):
    in_specs = (P("blk", "pool", None), P(None, ("blk", "pool"), None, None), P("blk", None))
    out_specs = P("blk", "pool", None)
    return jax.shard_map(body, mesh=mesh, in_specs=in_specs, out_specs=out_specs, check_vma=False)
```

```python
import functools
import math

import jax
import jax.numpy as jnp
from jax import lax
from jax.experimental import pallas as pl
from jax.experimental.pallas import tpu as pltpu
from jax.sharding import PartitionSpec as P

MESH = pl.DeviceIdType.MESH
NZ, NX, NC = 8, 2, 2
NH, NY = 2, 4
POOL = NH * NY
BS, D = 16, 128
NB, CAP = 96, 24
REQ, HEADS = 8, 16
ROWS = REQ * HEADS
SPLIT = (8, 6, 6, 4)
PEERS = ((1, 2), (1, 1), (1, 3), (1, 0), (0, 2), (0, 1), (0, 3))
PAIR = 2 * NX * ROWS
TILES = NZ // 2
PACK = D + 16
SCALE = math.log2(math.e) / math.sqrt(D)
LOG2E = math.log2(math.e)


def slot_of(dz):
    return 0 if dz == 0 else (2 * dz - 1 if dz <= NZ // 2 else 2 * (NZ - dz))


def step_of(slot):
    return (slot + 1) // 2 if slot % 2 else (NZ - slot // 2) % NZ


def packing(owner_ref, table_ref):
    owner = owner_ref[...]
    counts = [jnp.sum((owner == j).astype(jnp.int32), axis=1, keepdims=True) for j in range(POOL)]
    place = lax.broadcasted_iota(jnp.int32, (1, 128), 1)
    source = place
    ahead = None
    start = 0
    for size in SPLIT:
        for j in range(POOL):
            here = jnp.clip(counts[j] - start, 0, size)
            ahead = here if ahead is None else ahead + here
            source = source + jnp.where(place >= ahead, size - here, 0)
        start += size
    table_ref[...] = jnp.where(place < NB, jnp.minimum(source, POOL * CAP - 1), 0)


def kernel(
    q_ref, kv_ref, owner_ref, o_ref,
    owner_v, kv_v, qbuf, arrived, staged, packed, table_v, table_s, vt, scores, acc, peak, total,
    xsend, xrecv, zsend, zrecv,
    kv_ssem, kv_rsem, own_sem, first_sem, table_sem, qx_ssem, qx_rsem, qz_ssem, qz_rsem, c_ssem, c_rsem,
    xs_sem, xr_sem, zs_sem, zr_sem,
):
    blk, pool = lax.axis_index("blk"), lax.axis_index("pool")
    z, xl, core = blk // (NX * NC), (blk // NC) % NX, blk % NC
    xh, y = pool // NY, pool % NY

    def pool_peer(dx, dy):
        return (blk, ((xh + dx) % NH) * NY + (y + dy) % NY)

    def z_peer(dz):
        return (((z + dz) % NZ) * (NX * NC) + xl * NC + core, pool)

    x_peer = (z * (NX * NC) + (1 - xl) * NC + core, pool)
    core_peer = (z * (NX * NC) + xl * NC + (1 - core), pool)

    def remote(src, dst, ssem, rsem, device):
        return pltpu.make_async_remote_copy(
            src_ref=src, dst_ref=dst, send_sem=ssem, recv_sem=rsem, device_id=device, device_id_type=MESH
        )

    barrier = pltpu.get_barrier_semaphore()
    everyone = [z_peer(d) for d in range(1, NZ)] + [pool_peer(*p) for p in PEERS] + [x_peer, core_peer]
    for device in everyone:
        pl.semaphore_signal(barrier, inc=1, device_id=device, device_id_type=MESH)

    rows_in = pltpu.make_async_copy(q_ref, qbuf.at[0, 0], first_sem.at[0])
    rows_in.start()
    owners_in = pltpu.make_async_copy(owner_ref, owner_v, first_sem.at[1])
    owners_in.start()
    held = []
    start = 0
    for m, size in enumerate(SPLIT):
        copy = pltpu.make_async_copy(kv_ref.at[:, pl.ds(start, size)], kv_v.at[:, pl.ds(start, size)], own_sem.at[m])
        copy.start()
        held.append(copy)
        start += size
    rows_in.wait()
    pl.semaphore_wait(barrier, len(everyone))

    qx = remote(qbuf.at[0, 0], qbuf.at[0, 1], qx_ssem, qx_rsem, x_peer)
    qx.start()
    qz = [None] * (2 * NZ)
    order = [step_of(s) for s in range(1, NZ)]

    def send_rows(h):
        for d in order:
            at = slot_of(NZ - d)
            k = 2 * at + h
            qz[k] = remote(qbuf.at[0, h], qbuf.at[at, h], qz_ssem.at[k], qz_rsem.at[k], z_peer(d))
            qz[k].start()

    moves = []
    start = 0
    for m, size in enumerate(SPLIT):
        held[m].wait()
        part = []
        for i, (dx, dy) in enumerate(PEERS):
            device = pool_peer(dx, dy)
            copy = remote(
                kv_v.at[device[1], pl.ds(start, size)], arrived.at[pl.ds(start * POOL + pool * size, size)],
                kv_ssem.at[m, i], kv_rsem.at[m, i], device,
            )
            copy.start()
            part.append(copy)
        moves.append(part)
        start += size
        if m == 0:
            send_rows(0)
            qx.wait_recv()
            send_rows(1)
    owners_in.wait()
    packing(owner_v, table_v)
    to_smem = pltpu.make_async_copy(table_v, table_s, table_sem)
    to_smem.start()
    to_smem.wait()

    x_moves, z_moves = [None] * NZ, [None] * NZ

    def split3(v):
        high = v.astype(jnp.bfloat16)
        rest = v - high.astype(jnp.float32)
        mid = rest.astype(jnp.bfloat16)
        low = (rest - mid.astype(jnp.float32)).astype(jnp.bfloat16)
        return high, mid, low

    def put(ref, s, value, lse):
        ref[s, pl.ds(0, D)] = value.astype(jnp.bfloat16)
        parts = jnp.concatenate([p.astype(jnp.float32) for p in split3(lse)] + [jnp.zeros((13, ROWS), jnp.float32)], axis=0)
        ref[s, pl.ds(D, 16)] = parts.astype(jnp.bfloat16)

    def get(ref, s):
        tail = ref[s, pl.ds(D, 16)].astype(jnp.float32)
        return ref[s, pl.ds(0, D)].astype(jnp.float32), tail[0:1] + tail[1:2] + tail[2:3]

    def combine(s):
        x_moves[s].wait_recv()
        t, lanes = s // 2, pl.ds((s % 2) * NX * ROWS, ROWS)
        mine, lse_a = acc[t, :, lanes], peak[t, :, lanes]
        theirs, lse_b = get(xrecv, s)
        top = jnp.maximum(lse_a, lse_b)
        wa, wb = jnp.exp2(lse_a - top), jnp.exp2(lse_b - top)
        norm = wa + wb
        inv = 1.0 / norm
        put(zsend, s, mine * (wa * inv) + theirs * (wb * inv), top + jnp.log(norm) * LOG2E)
        if s > 0:
            z_moves[s] = remote(zsend.at[s], zrecv.at[s], zs_sem.at[s], zr_sem.at[s], z_peer(step_of(s)))
            z_moves[s].start()

    def attend(turn, base, blocks, final=False):
        first = turn == 0
        tokens = blocks * BS
        side = turn % 2
        vt[side, :, pl.ds(0, tokens)] = jnp.swapaxes(packed[pl.ds(base, blocks), :, D:].reshape(tokens, D), 0, 1)

        def score(t, b):
            if first:
                for s in (2 * t, 2 * t + 1):
                    if s > 0:
                        qz[2 * s].wait_recv()
                        qz[2 * s + 1].wait_recv()
            keys = packed[pl.ds(base, blocks), :, :D].reshape(tokens, D)
            rows = qbuf[pl.ds(2 * t, 2)].reshape(PAIR, D)
            scores[b, pl.ds(0, tokens)] = lax.dot_general(
                keys, rows, (((1,), (1,)), ((), ())), preferred_element_type=jnp.float32
            )

        def soft(t, b):
            s = scores[b, pl.ds(0, tokens)]
            high = jnp.max(s, axis=0, keepdims=True)
            if not first:
                previous = peak[t]
                high = jnp.maximum(high, previous)
            high_c = high * SCALE
            weight = jnp.exp2(s * SCALE - high_c)
            mass = jnp.sum(weight, axis=0, keepdims=True)
            out = jnp.dot(vt[side, :, pl.ds(0, tokens)], weight.astype(jnp.bfloat16), preferred_element_type=jnp.float32)
            if not first:
                keep = jnp.exp2(previous * SCALE - high_c)
                mass = mass + keep * total[t]
                out = out + keep * acc[t]
            if not final:
                peak[t] = high
                total[t] = mass
                acc[t] = out
                return
            out = out * (1.0 / mass)
            lse = high_c + jnp.log(mass) * LOG2E
            acc[t] = out
            peak[t] = lse
            for h in (1, 0):
                slot = 2 * t + h
                lanes = slice((2 * h + 1) * ROWS, (2 * h + 2) * ROWS)
                put(xsend, slot, out[:, lanes], lse[:, lanes])
                x_moves[slot] = remote(xsend.at[slot], xrecv.at[slot], xs_sem.at[slot], xr_sem.at[slot], x_peer)
                x_moves[slot].start()

        tiles = list(range(TILES))
        if final:
            tiles = tiles[::-1]
        score(tiles[0], 0)
        for i, t in enumerate(tiles):
            if i + 1 < TILES:
                score(tiles[i + 1], (i + 1) % 2)
            soft(t, i % 2)

    swaps = []
    start = 0
    for m, size in enumerate(SPLIT):
        blocks = size * POOL // 2
        for copy in moves[m]:
            copy.wait_recv()
        staged[pl.ds(start * POOL, size * POOL)] = arrived[pl.ds(start * POOL, size * POOL)]
        staged[pl.ds(start * POOL + pool * size, size)] = kv_v[pool, pl.ds(start, size)]
        base = start * POOL
        for p in range(blocks):
            packed[base + p] = staged[table_s[0, start * POOL // 2 + p]]
        swap = remote(
            packed.at[pl.ds(base, blocks)], packed.at[pl.ds(base + blocks, blocks)], c_ssem.at[m], c_rsem.at[m], core_peer
        )
        swap.start()
        swaps.append(swap)
        if m == 0:
            attend(0, 0, blocks)
        else:
            swaps[m - 1].wait_recv()
            attend(m, base - before, before + blocks)
        before = blocks
        start += size
    swaps[-1].wait_recv()
    attend(len(SPLIT), base + blocks, blocks, final=True)
    for s in range(NZ - 1, -1, -1):
        combine(s)

    values, logs = [], []
    for s in range(NZ):
        if s > 0:
            z_moves[s].wait_recv()
        value, lse = get(zsend if s == 0 else zrecv, s)
        values.append(value)
        logs.append(lse)
    top = functools.reduce(jnp.maximum, logs)
    weights = [jnp.exp2(v - top) for v in logs]
    inv = 1.0 / functools.reduce(jnp.add, weights)
    result = functools.reduce(jnp.add, [v * (w * inv) for v, w in zip(values, weights)])
    o_ref[...] = jnp.swapaxes(result, 0, 1).astype(jnp.bfloat16).reshape(o_ref.shape)

    qx.wait_send()
    for copy in qz[2:]:
        copy.wait_send()
    for part in moves:
        for copy in part:
            copy.wait_send()
    for copy in swaps + x_moves + z_moves[1:]:
        copy.wait_send()


def body(queries, kv_cache, block_owner):
    widest = max(a + b for a, b in zip(SPLIT, SPLIT[1:])) * POOL // 2 * BS
    dma = pltpu.SemaphoreType.DMA
    return pl.pallas_call(
        kernel,
        out_shape=pltpu.VMEM(queries.shape, queries.dtype),
        in_specs=[
            pl.BlockSpec(memory_space=pltpu.HBM),
            pl.BlockSpec(memory_space=pltpu.HBM),
            pl.BlockSpec(memory_space=pltpu.HBM),
        ],
        out_specs=pl.BlockSpec(memory_space=pltpu.VMEM),
        scratch_shapes=[
            pltpu.VMEM((1, NB), jnp.int32),
            pltpu.VMEM((POOL, CAP, BS, 2 * D), jnp.bfloat16),
            pltpu.VMEM((NZ, NX, REQ, HEADS, D), jnp.bfloat16),
            pltpu.VMEM((POOL * CAP, BS, 2 * D), jnp.bfloat16),
            pltpu.VMEM((POOL * CAP, BS, 2 * D), jnp.bfloat16),
            pltpu.VMEM((2 * NB, BS, 2 * D), jnp.bfloat16),
            pltpu.VMEM((1, 128), jnp.int32),
            pltpu.SMEM((1, 128), jnp.int32),
            pltpu.VMEM((2, D, widest), jnp.bfloat16),
            pltpu.VMEM((2, widest, PAIR), jnp.float32),
            pltpu.VMEM((TILES, D, PAIR), jnp.float32),
            pltpu.VMEM((TILES, 1, PAIR), jnp.float32),
            pltpu.VMEM((TILES, 1, PAIR), jnp.float32),
            pltpu.VMEM((NZ, PACK, ROWS), jnp.bfloat16),
            pltpu.VMEM((NZ, PACK, ROWS), jnp.bfloat16),
            pltpu.VMEM((NZ, PACK, ROWS), jnp.bfloat16),
            pltpu.VMEM((NZ, PACK, ROWS), jnp.bfloat16),
            dma((len(SPLIT), len(PEERS))),
            dma((len(SPLIT), len(PEERS))),
            dma((len(SPLIT),)),
            dma((2,)),
            dma,
            dma,
            dma,
            dma((2 * NZ,)),
            dma((2 * NZ,)),
            dma((len(SPLIT),)),
            dma((len(SPLIT),)),
            dma((NZ,)),
            dma((NZ,)),
            dma((NZ,)),
            dma((NZ,)),
        ],
        compiler_params=pltpu.CompilerParams(
            collective_id=0, has_side_effects=True, vmem_limit_bytes=56 * 1024 * 1024
        ),
        cost_estimate=pl.CostEstimate(flops=3_300_000_000, bytes_accessed=4_000_000, transcendentals=6_300_000),
    )(queries, kv_cache, block_owner.reshape(1, NB))


def solution(mesh):
    in_specs = (P("blk", "pool", None), P(None, ("blk", "pool"), None, None), P("blk", None))
    out_specs = P("blk", "pool", None)
    return jax.shard_map(body, mesh=mesh, in_specs=in_specs, out_specs=out_specs, check_vma=False)
```
